512 devices in a mesh: clus: 32 (over y, x_lo, core), head: 16 (over z, x_hi).
Axes of the slice: x: 4 (x_hi: 2, x_lo: 2; x = x_hi * 2 + x_lo), y: 8, z: 8, core: 2. Of those that a mesh axis runs over, the one named last changes fastest.
Arguments:
- node_queries: bfloat16 [131072, 1024], P(('clus', 'head')), may hold values from -8 to 8
- node_keys: bfloat16 [131072, 1024], P(('clus', 'head')), may hold values from -8 to 8
- node_values: bfloat16 [131072, 1024], P(('clus', 'head')), may hold values from -6 to 6
- matchings: int32 [3, 32], replicated, may hold values from 0 to 31, as said below
- patterns: int32 [32, 32, 12], P('clus'), may hold values from 0 to 127, as said below
- out_gain: float32 [1024], replicated, may hold values from 0.5 to 1.5
Outputs:
- attended: bfloat16 [131072, 1024], P(('clus', 'head'))
The draws below stay inside these ranges and needn't reach their ends.
Inputs may be any that keep to these rules, and one draw needn't show every extreme that they name: Each row is a perfect matching: matchings[j, c] != c and matchings[j, matchings[j, c]] == c. `patterns`: for every cluster and query block, entries s * 3 to (s + 1) * 3 - 1 are 3 different blocks of source s, that is numbers from s * 32 to (s + 1) * 32 - 1.
All inputs are finite; a program needn't handle non-finite values.
Results may differ from the reference program's by a relative error of at most 0.0057.
Values may be sent and summed in bfloat16 or wider, within the bound.
A program may use at most 64 MiB of HBM per device.

```python
import math
import jax
import jax.numpy as jnp
from jax import lax

D = 1024
HEAD_DIM = 64
CN = 4096
BLOCK = 128
PER_SRC = 3
MATCHINGS = 3
CLUSTERS = 32
NODES = 131072
BLOCKS = 32
NB = 12


def draw_node_queries(key, part):
    normal_draw = jax.random.normal(jax.random.fold_in(key, 21), (NODES, D), jnp.float32)
    return jnp.clip(normal_draw, -6.0, 6.0).astype(jnp.bfloat16)


def draw_node_keys(key, part):
    normal_draw = jax.random.normal(jax.random.fold_in(key, 31), (NODES, D), jnp.float32)
    return jnp.clip(normal_draw, -6.0, 6.0).astype(jnp.bfloat16)


def draw_matchings(key, part):
    rows_out = []
    for which in range(MATCHINGS):
        shuffled = jax.random.permutation(jax.random.fold_in(key, 41 + which), CLUSTERS).astype(jnp.int32)
        first_half = shuffled[0::2]
        second_half = shuffled[1::2]
        partner = jnp.zeros((CLUSTERS,), jnp.int32).at[first_half].set(second_half).at[second_half].set(first_half)
        rows_out.append(partner)
    return jnp.stack(rows_out)


def draw_patterns(key, part):
    total = CLUSTERS * BLOCKS * (MATCHINGS + 1)
    subkeys = jax.random.split(jax.random.fold_in(key, 51), total)
    picks = jax.vmap(lambda subkey: jax.random.permutation(subkey, BLOCKS)[:PER_SRC])(subkeys)
    picks = picks.reshape(CLUSTERS, BLOCKS, MATCHINGS + 1, PER_SRC).astype(jnp.int32)
    offsets = (jnp.arange(MATCHINGS + 1, dtype=jnp.int32) * BLOCKS)[None, None, :, None]
    return (picks + offsets).reshape(CLUSTERS, BLOCKS, NB)


def steps_of(key, extent, cuts, least, largest):
    factor_of = 1.0
    for axis_at, shards_of in cuts:
        steps = jax.random.uniform(jax.random.fold_in(jax.random.fold_in(key, 6), axis_at), (shards_of,), jnp.float32, least / len(cuts), largest / len(cuts))
        factor_of = factor_of * jnp.repeat(jnp.exp(steps), extent[axis_at] // shards_of).reshape((-1,) + (1,) * (len(extent) - 1 - axis_at))
    return factor_of


def noise(rng, shape, width, bound, pieces=(), held_as=jnp.bfloat16):
    values = width * jax.random.normal(rng, shape, jnp.float32)
    if pieces:
        values = values * steps_of(rng, shape, pieces, -0.22, 0.18)
    return jnp.clip(values, -bound, bound).astype(held_as)


def setup_inputs(seed: int = 0) -> dict:
    arg_keys = jax.random.split(jax.random.key(seed), 7)
    node_queries = draw_node_queries(jax.random.fold_in(arg_keys[6], 71), 0)
    node_keys = draw_node_keys(jax.random.fold_in(arg_keys[6], 71), 0)
    node_values = noise(arg_keys[2], (NODES, D), 1.0, 6.0, ((0, 512),))
    matchings = draw_matchings(jax.random.fold_in(arg_keys[6], 71), 0)
    patterns = draw_patterns(jax.random.fold_in(arg_keys[6], 71), 0)
    out_gain = jnp.clip(1.0 + 0.1 * jax.random.normal(arg_keys[5], (D,), jnp.float32), 0.5, 1.5)
    return dict(node_queries=node_queries, node_keys=node_keys, node_values=node_values, matchings=matchings, patterns=patterns, out_gain=out_gain)


group_blocks = 4

def attend_group(query_group, key_group, value_group):
    score_scale = 1.0 / math.sqrt(HEAD_DIM)
    scores = jnp.einsum('bqhd,bkhd->bhqk', query_group.astype(jnp.float32), key_group.astype(jnp.float32)) * score_scale
    maximum = lax.optimization_barrier(jnp.max(scores, axis=-1, keepdims=True))
    powers = jnp.exp(scores - maximum)
    weights = (powers / lax.optimization_barrier(jnp.sum(powers, axis=-1, keepdims=True))).astype(jnp.bfloat16)
    mixed_rows = jnp.einsum('bhqk,bkhd->bqhd', weights.astype(jnp.float32), value_group.astype(jnp.float32))
    return mixed_rows.astype(jnp.bfloat16)

def attend_cluster(query_rows, key_rows, value_rows, pattern):
    row_count = query_rows.shape[0]
    feature_width = query_rows.shape[1]
    head_count = feature_width // HEAD_DIM
    groups = pattern.shape[0] // group_blocks
    query_groups = query_rows.reshape(groups, group_blocks, BLOCK, head_count, HEAD_DIM)
    key_blocks = key_rows.reshape(-1, BLOCK, head_count, HEAD_DIM)
    value_blocks = value_rows.reshape(-1, BLOCK, head_count, HEAD_DIM)
    pattern_groups = pattern.reshape(groups, group_blocks, -1)

    def one_group(inputs):
        query_group, chosen = inputs
        key_group = jnp.take(key_blocks, chosen, axis=0).reshape(group_blocks, -1, head_count, HEAD_DIM)
        value_group = jnp.take(value_blocks, chosen, axis=0).reshape(group_blocks, -1, head_count, HEAD_DIM)
        return attend_group(query_group, key_group, value_group)
    mixed_rows = lax.map(one_group, (query_groups, pattern_groups))
    return mixed_rows.reshape(row_count, feature_width)

def reference(node_queries, node_keys, node_values, matchings, patterns, out_gain):
    cluster_queries = node_queries.reshape(CLUSTERS, CN, D)
    cluster_keys = node_keys.reshape(CLUSTERS, CN, D)
    cluster_values = node_values.reshape(CLUSTERS, CN, D)

    def one_cluster(cluster):
        partners = matchings[:, cluster]
        key_rows = jnp.concatenate([cluster_keys[cluster][None], jnp.take(cluster_keys, partners, axis=0)], axis=0).reshape(-1, D)
        value_rows = jnp.concatenate([cluster_values[cluster][None], jnp.take(cluster_values, partners, axis=0)], axis=0).reshape(-1, D)
        return attend_cluster(cluster_queries[cluster], key_rows, value_rows, patterns[cluster])
    mixed_rows = lax.map(one_cluster, jnp.arange(CLUSTERS, dtype=jnp.int32))
    mixed_rows = mixed_rows.reshape(-1, D).astype(jnp.float32)
    mean_square = lax.optimization_barrier(jnp.mean(mixed_rows * mixed_rows, axis=-1, keepdims=True))
    return (mixed_rows * lax.rsqrt(mean_square + 1e-06) * out_gain.astype(jnp.float32)).astype(jnp.bfloat16)
```

```python
import functools
import math

import jax
import jax.numpy as jnp
from jax import lax
from jax.experimental import pallas as pl
from jax.experimental.pallas import tpu as pltpu
from jax.sharding import PartitionSpec as P

HEAD_DIM = 64
BLOCK = 128
LANES = 128
PARTS = 2
ROWS = BLOCK // PARTS
PHASES = 2 * PARTS
NEAR = 4
MESH = pl.DeviceIdType.MESH


def attention_kernel(
    dims,
    tile_ref,
    half_ref,
    match_ref,
    q_ref,
    k_ref,
    v_ref,
    gain_ref,
    out_ref,
    packed,
    packed_q,
    staged,
    queries,
    powers,
    scores,
    masks,
    mixed_out,
    mixed_in,
    *rest,
):
    heads, ring, near, chosen = dims
    gathered = rest[:PHASES]
    selected = rest[PHASES : 2 * PHASES]
    (
        first_send,
        first_send_same,
        first_recv,
        ring_send,
        ring_recv,
        own_send,
        own_recv,
        partner_send,
        partner_recv,
        q_send,
        q_recv,
        mixed_send,
        mixed_recv,
    ) = rest[2 * PHASES :]
    tiles = heads // near
    sources = 4
    far = ring // 2
    sub = near // 2
    clus = lax.axis_index("clus")
    h = lax.axis_index("head")
    y = clus // near
    u = clus % near
    home = h % near
    same = home == u

    def copy(src, dst, send, recv, to_clus, to_head):
        return pltpu.make_async_remote_copy(
            src_ref=src,
            dst_ref=dst,
            send_sem=send,
            recv_sem=recv,
            device_id={"clus": to_clus, "head": to_head},
            device_id_type=MESH,
        )

    def arrived(ref, sem):
        pltpu.make_async_copy(ref, ref, sem).wait()

    barrier = pltpu.get_barrier_semaphore()

    def greet(to_clus, to_head):
        pl.semaphore_signal(
            barrier, inc=1, device_id={"clus": to_clus, "head": to_head}, device_id_type=MESH
        )

    def greet_first(i, carry):
        to_clus = y * near + i // tiles
        to_head = u + near * (i % tiles)

        @pl.when(jnp.logical_or(to_clus != clus, to_head != h))
        def _():
            greet(to_clus, to_head)

        return carry

    def greet_head(r, carry):
        greet(clus, (h + r) % heads)
        return carry

    lax.fori_loop(0, near * tiles, greet_first, 0)
    lax.fori_loop(1, heads, greet_head, 0)
    for r in range(1, near):
        greet(y * near + (u + r) % near, h)
    above = ((y + 1) % ring) * near + u
    below = ((y + ring - 1) % ring) * near + u
    greet(above, h)
    greet(below, h)

    def pack(ref, put):
        for t in range(heads // 2):
            first = ref[0:BLOCK, t * LANES : (t + 1) * LANES]
            second = ref[BLOCK : 2 * BLOCK, t * LANES : (t + 1) * LANES]
            put(
                2 * t,
                jnp.concatenate([first[:, :HEAD_DIM], second[:, :HEAD_DIM]], axis=1),
            )
            put(
                2 * t + 1,
                jnp.concatenate([first[:, HEAD_DIM:], second[:, HEAD_DIM:]], axis=1),
            )

    def put_rows(which):
        def put(head, tile):
            for part in range(PARTS):
                packed[which * PARTS + part, head] = tile[part * ROWS : (part + 1) * ROWS]

        return put

    def put_q(head, tile):
        packed_q[head] = tile

    pack(k_ref, put_rows(0))
    lane = lax.broadcasted_iota(jnp.int32, (16, LANES), 1)
    masks[0] = jnp.where(lane < HEAD_DIM, 1.0, 0.0).astype(masks.dtype)
    masks[1] = jnp.where(lane < HEAD_DIM, 0.0, 1.0).astype(masks.dtype)

    itself = jnp.where(same, 1, 0)
    pl.semaphore_wait(barrier, (near * tiles - itself) + (heads - 1) + (near - 1) + 2)

    def first_copy(p, r):
        g = (h + r) % heads
        return copy(
            packed.at[p, g],
            gathered[p].at[clus, h // near],
            first_send.at[p],
            first_recv.at[p],
            y * near + home,
            g,
        )

    def first_copy_same(p):
        return copy(
            packed.at[p, h],
            gathered[p].at[clus, h // near],
            first_send_same.at[p],
            first_recv.at[p],
            y * near + home,
            h,
        )

    def first_start(p):
        @pl.when(same)
        def _():
            pltpu.make_async_copy(
                packed.at[p, h], gathered[p].at[clus, h // near], first_recv.at[p]
            ).start()

        @pl.when(jnp.logical_not(same))
        def _():
            first_copy_same(p).start()

        def step(r, carry):
            first_copy(p, r).start()
            return carry

        lax.fori_loop(1, heads, step, 0)

    def q_start():
        pltpu.make_async_copy(packed_q.at[h], queries.at[h], q_recv).start()

        def step(r, carry):
            g = (h + r) % heads
            copy(packed_q.at[g], queries.at[h], q_send, q_recv, clus, g).start()
            return carry

        lax.fori_loop(1, heads, step, 0)

    def ring_copy(p, way, step, part):
        if way == 0:
            slot, to = (y + ring - (step - 1)) % ring, above
        else:
            slot, to = (y + step - 1) % ring, below
        ref = gathered[p].at[pl.ds(slot * near + part * sub, sub)]
        return copy(
            ref,
            ref,
            ring_send.at[p, way, step - 1, part],
            ring_recv.at[p, way, step - 1, part],
            to,
            h,
        )

    def ring_wait(p, way, step, part):
        slot = (y + ring - step) % ring if way == 0 else (y + step) % ring
        arrived(
            gathered[p].at[pl.ds(slot * near + part * sub, sub)],
            ring_recv.at[p, way, step - 1, part],
        )

    def own_copy(p, r):
        to = y * near + (u + r) % near
        return copy(
            gathered[p].at[to],
            selected[p].at[pl.ds(u * sources * tiles, tiles)],
            own_send.at[p, r - 1],
            own_recv.at[p, r - 1],
            to,
            h,
        )

    def partner_copy(p, r):
        return copy(
            staged.at[p, r - 1],
            selected[p].at[pl.ds((u * sources + 1) * tiles, (sources - 1) * tiles)],
            partner_send.at[p, r - 1],
            partner_recv.at[p, r - 1],
            y * near + (u + r) % near,
            h,
        )

    def enter(p):
        arrived(gathered[p].at[pl.ds(y * near, near)], first_recv.at[p])
        for part in range(2):
            for way in range(2):
                ring_copy(p, way, 1, part).start()
        for r in range(1, near):
            own_copy(p, r).start()

    def forward(p, step, between=lambda: None):
        for part in range(2):
            for way in range(2):
                ring_wait(p, way, step - 1, part)
                if step < far or part == way:
                    ring_copy(p, way, step, part).start()
            between()

    def leave(p):
        for way in range(2):
            ring_wait(p, way, far, way)
        for r in range(1, near):
            to = y * near + (u + r) % near
            for j in range(sources - 1):
                staged[p, r - 1, j * tiles : (j + 1) * tiles] = gathered[p][
                    match_ref[j * ring * near + to]
                ]
            partner_copy(p, r).start()
        selected[p][pl.ds(u * sources * tiles, tiles)] = gathered[p][clus]
        for j in range(sources - 1):
            selected[p][pl.ds((u * sources + 1 + j) * tiles, tiles)] = gathered[p][
                match_ref[j * ring * near + clus]
            ]

    def settle(p):
        for r in range(1, near):
            from_u = (u + near - r) % near
            arrived(
                selected[p].at[pl.ds(from_u * sources * tiles, tiles)], own_recv.at[p, r - 1]
            )
            arrived(
                selected[p].at[pl.ds((from_u * sources + 1) * tiles, (sources - 1) * tiles)],
                partner_recv.at[p, r - 1],
            )

    def masked_rows(parts, b):
        rows = []
        for n in range(chosen):
            tile = tile_ref[b * chosen + n]
            mask = masks[half_ref[b * chosen + n]]
            for part in parts:
                block = part[tile].reshape(ROWS // 16, 16, LANES)
                rows.append((block * mask[None]).reshape(ROWS, LANES))
        return jnp.concatenate(rows, axis=0)

    exponent_scale = 1.0 / (math.sqrt(HEAD_DIM) * math.log(2.0))

    def weigh(b, query):
        keys = masked_rows(selected[:PARTS], b)
        scores[...] = lax.dot_general(
            query, keys, (((1,), (1,)), ((), ())), preferred_element_type=jnp.float32
        )
        step = 16
        for i in range(BLOCK // step):
            s = scores[i * step : (i + 1) * step, :]
            top = jnp.max(s, axis=1, keepdims=True)
            power = jnp.exp2((s - top) * exponent_scale)
            total = jnp.sum(power, axis=1, keepdims=True)
            powers[b, i * step : (i + 1) * step, :] = (power * (1.0 / total)).astype(jnp.bfloat16)

    def weigh_pair(w, carry):
        pair = queries[w]
        low, high = pair[:, :HEAD_DIM], pair[:, HEAD_DIM:]
        weigh(2 * w, jnp.concatenate([low, low], axis=1))
        weigh(2 * w + 1, jnp.concatenate([high, high], axis=1))
        return carry

    done = [0]

    def weigh_some(count):
        stop = min(done[0] + count, heads)
        if stop > done[0]:
            lax.fori_loop(done[0], stop, weigh_pair, 0)
        done[0] = stop

    def mix(b):
        values = masked_rows(selected[PARTS:], b)
        both = jnp.dot(powers[b], values, preferred_element_type=jnp.float32)
        return both + jnp.concatenate([both[:, HEAD_DIM:], both[:, :HEAD_DIM]], axis=1)

    def mix_pair(w):
        low, high = mix(2 * w), mix(2 * w + 1)
        lanes = lax.broadcasted_iota(jnp.int32, (BLOCK, LANES), 1)
        mixed_out[w] = jnp.where(lanes < HEAD_DIM, low, high).astype(jnp.bfloat16)

    def mix_send(r, carry):
        w = (h + r) % heads
        mix_pair(w)
        copy(mixed_out.at[w], mixed_in.at[h], mixed_send, mixed_recv, clus, w).start()
        return carry

    for part in range(PARTS):
        first_start(part)
    pack(v_ref, put_rows(1))
    pack(q_ref, put_q)
    for p in range(PHASES):
        enter(p)
        if p < PARTS:
            first_start(PARTS + p)
        if p == PARTS - 1:
            q_start()
        if p > 0:
            forward(p - 1, far)
        if p == PHASES - 1:
            for part in range(PARTS):
                settle(part)
            arrived(queries, q_recv)
            weigh_some(4)
        for step in range(2, far):
            forward(p, step, functools.partial(weigh_some, 2 if p == PHASES - 1 else 0))
            if step == 2 and p > 0:
                leave(p - 1)
    forward(PHASES - 1, far, functools.partial(weigh_some, 2))
    leave(PHASES - 1)
    weigh_some(heads)
    for part in range(PARTS):
        settle(PARTS + part)

    lax.fori_loop(1, heads, mix_send, 0)
    mix_pair(h)
    pltpu.make_async_copy(mixed_out.at[h], mixed_in.at[h], mixed_recv).start()

    for p in range(PHASES):
        arrived(packed.at[p, 0 : heads - 1], first_send.at[p])

        @pl.when(jnp.logical_not(same))
        def _():
            first_copy_same(p).wait_send()

        for step in range(1, far + 1):
            for part in range(2):
                for way in range(2):
                    if step < far or part == way:
                        ring_copy(p, way, step, part).wait_send()
        for r in range(1, near):
            own_copy(p, r).wait_send()
            partner_copy(p, r).wait_send()
    arrived(packed_q.at[0 : heads - 1], q_send)
    arrived(mixed_out.at[0 : heads - 1], mixed_send)

    arrived(mixed_in, mixed_recv)
    step = 32
    for i in range(BLOCK // step):
        rows = slice(i * step, (i + 1) * step)
        firsts, seconds = [], []
        for t in range(heads // 2):
            even = mixed_in[2 * t, rows]
            odd = mixed_in[2 * t + 1, rows]
            firsts.append(jnp.concatenate([even[:, :HEAD_DIM], odd[:, :HEAD_DIM]], axis=1))
            seconds.append(jnp.concatenate([even[:, HEAD_DIM:], odd[:, HEAD_DIM:]], axis=1))
        for at, group in ((0, firsts), (BLOCK, seconds)):
            whole = jnp.concatenate(group, axis=1).astype(jnp.float32)
            mean_square = jnp.mean(whole * whole, axis=1, keepdims=True)
            normed = whole * lax.rsqrt(mean_square + 1e-06) * gain_ref[...]
            out_ref[at + i * step : at + (i + 1) * step, :] = normed.astype(out_ref.dtype)


def local(shape, node_queries, node_keys, node_values, matchings, patterns, out_gain):
    clusters, heads = shape
    near = NEAR if clusters >= 4 * NEAR else 2
    ring = clusters // near
    blocks, chosen = patterns.shape[1:]
    tiles = heads // near
    far = ring // 2
    width = node_queries.shape[1]
    pattern = patterns.reshape(-1)
    source = pattern // blocks
    pair = (pattern % blocks) // 2
    tile_at = ((pair % near) * 4 + source) * tiles + pair // near
    half = pattern % 2
    dtype = node_queries.dtype
    vmem = pl.BlockSpec(memory_space=pltpu.VMEM)
    smem = pl.BlockSpec(memory_space=pltpu.SMEM)
    dma = pltpu.SemaphoreType.DMA
    scratch = [
        pltpu.VMEM((PHASES, heads, ROWS, LANES), dtype),
        pltpu.VMEM((heads, BLOCK, LANES), dtype),
        pltpu.VMEM((PHASES, near - 1, 3 * tiles, ROWS, LANES), dtype),
        pltpu.VMEM((heads, BLOCK, LANES), dtype),
        pltpu.VMEM((blocks, BLOCK, chosen * BLOCK), dtype),
        pltpu.VMEM((BLOCK, chosen * BLOCK), jnp.float32),
        pltpu.VMEM((2, 16, LANES), dtype),
        pltpu.VMEM((heads, BLOCK, LANES), dtype),
        pltpu.VMEM((heads, BLOCK, LANES), dtype),
    ]
    scratch += [pltpu.VMEM((clusters, tiles, ROWS, LANES), dtype)] * PHASES
    scratch += [pltpu.VMEM((near * 4 * tiles, ROWS, LANES), dtype)] * PHASES
    scratch += [
        dma((PHASES,)),
        dma((PHASES,)),
        dma((PHASES,)),
        dma((PHASES, 2, far, 2)),
        dma((PHASES, 2, far, 2)),
        dma((PHASES, near - 1)),
        dma((PHASES, near - 1)),
        dma((PHASES, near - 1)),
        dma((PHASES, near - 1)),
        dma,
        dma,
        dma,
        dma,
    ]
    return pl.pallas_call(
        functools.partial(attention_kernel, (heads, ring, near, chosen)),
        out_shape=jax.ShapeDtypeStruct(node_queries.shape, dtype),
        in_specs=[smem] * 3 + [vmem] * 4,
        out_specs=vmem,
        scratch_shapes=scratch,
        compiler_params=pltpu.CompilerParams(
            collective_id=0, has_side_effects=True, vmem_limit_bytes=56 * 1024 * 1024
        ),
    )(
        tile_at,
        half,
        matchings.reshape(-1),
        node_queries,
        node_keys,
        node_values,
        out_gain.reshape(1, width),
    )


def solution(mesh):
    in_specs = (
        P(("clus", "head"), None),
        P(("clus", "head"), None),
        P(("clus", "head"), None),
        P(),
        P("clus", None, None),
        P(),
    )
    out_specs = P(("clus", "head"), None)
    return jax.shard_map(
        functools.partial(local, (mesh.shape["clus"], mesh.shape["head"])),
        mesh=mesh,
        in_specs=in_specs,
        out_specs=out_specs,
        check_vma=False,
    )
```

```python
import functools
import math

import jax
import jax.numpy as jnp
from jax import lax
from jax.experimental import pallas as pl
from jax.experimental.pallas import tpu as pltpu
from jax.sharding import PartitionSpec as P

HEAD_DIM = 64
BLOCK = 128
LANES = 128
PARTS = 4
ROWS = BLOCK // PARTS
PHASES = 2 * PARTS
SIDES = 2
SIDE = HEAD_DIM // SIDES
NEAR = 4
MESH = pl.DeviceIdType.MESH


def attention_kernel(
    dims,
    pattern_ref,
    match_ref,
    q_hbm,
    k_hbm,
    v_hbm,
    out_ref,
    q_ref,
    k_ref,
    v_ref,
    packed,
    packed_q,
    staged,
    queries,
    powers,
    scores,
    masks,
    mixed_out,
    mixed_in,
    ahead,
    tile_ref,
    half_ref,
    *rest,
):
    heads, ring, near, chosen, blocks = dims
    gathered = rest[:PHASES]
    selected = rest[PHASES : 2 * PHASES]
    (
        load,
        first_send,
        first_send_same,
        first_recv,
        ring_send,
        ring_recv,
        own_send,
        own_recv,
        partner_send,
        partner_recv,
        q_send,
        q_recv,
        mixed_send,
        mixed_recv,
    ) = rest[2 * PHASES :]
    tiles = heads // near
    sources = 4
    far = ring // 2
    clus = lax.axis_index("clus")
    h = lax.axis_index("head")
    y = clus // near
    u = clus % near
    home = h % near
    same = home == u

    def copy(src, dst, send, recv, to_clus, to_head):
        return pltpu.make_async_remote_copy(
            src_ref=src,
            dst_ref=dst,
            send_sem=send,
            recv_sem=recv,
            device_id={"clus": to_clus, "head": to_head},
            device_id_type=MESH,
        )

    def arrived(ref, sem):
        pltpu.make_async_copy(ref, ref, sem).wait()

    loads = [
        pltpu.make_async_copy(src, dst, load.at[i])
        for i, (src, dst) in enumerate(((k_hbm, k_ref), (v_hbm, v_ref), (q_hbm, q_ref)))
    ]
    for one in loads:
        one.start()

    barrier = pltpu.get_barrier_semaphore()

    def greet(to_clus, to_head):
        pl.semaphore_signal(
            barrier, inc=1, device_id={"clus": to_clus, "head": to_head}, device_id_type=MESH
        )

    def greet_first(i, carry):
        to_clus = y * near + i // tiles
        to_head = u + near * (i % tiles)

        @pl.when(jnp.logical_or(to_clus != clus, to_head != h))
        def _():
            greet(to_clus, to_head)

        return carry

    def greet_head(r, carry):
        greet(clus, (h + r) % heads)
        return carry

    lax.fori_loop(0, near * tiles, greet_first, 0)
    lax.fori_loop(1, heads, greet_head, 0)
    for r in range(1, near):
        greet(y * near + (u + r) % near, h)
    above = ((y + 1) % ring) * near + u
    below = ((y + ring - 1) % ring) * near + u
    greet(above, h)
    greet(below, h)

    def pack(ref, put):
        for t in range(heads // 2):
            first = ref[0:BLOCK, t * LANES : (t + 1) * LANES]
            second = ref[BLOCK : 2 * BLOCK, t * LANES : (t + 1) * LANES]
            put(
                2 * t,
                jnp.concatenate([first[:, :HEAD_DIM], second[:, :HEAD_DIM]], axis=1),
            )
            put(
                2 * t + 1,
                jnp.concatenate([first[:, HEAD_DIM:], second[:, HEAD_DIM:]], axis=1),
            )

    def put_keys(head, tile):
        for part in range(PARTS):
            packed[part, head] = tile[part * ROWS : (part + 1) * ROWS]

    def put_values(head, tile):
        middle = BLOCK // 2
        for side in range(SIDES):
            pieces = [
                tile[rows, at + side * SIDE : at + (side + 1) * SIDE]
                for at in (0, HEAD_DIM)
                for rows in (slice(0, middle), slice(middle, BLOCK))
            ]
            wide = jnp.concatenate(pieces, axis=1)
            for part in range(2):
                packed[PARTS + 2 * side + part, head] = wide[part * ROWS : (part + 1) * ROWS]

    def put_q(head, tile):
        packed_q[head] = tile

    loads[0].wait()
    pack(k_ref, put_keys)
    lane = lax.broadcasted_iota(jnp.int32, (16, LANES), 1)
    for i in range(2):
        masks[i] = jnp.where(lane // HEAD_DIM == i, 1.0, 0.0).astype(masks.dtype)
    for i in range(4):
        masks[2 + i] = jnp.where(lane // SIDE == i, 1.0, 0.0).astype(masks.dtype)

    itself = jnp.where(same, 1, 0)
    pl.semaphore_wait(barrier, (near * tiles - itself) + (heads - 1) + (near - 1) + 2)

    def first_copy(p, r):
        g = (h + r) % heads
        return copy(
            packed.at[p, g],
            gathered[p].at[clus, h // near],
            first_send.at[p],
            first_recv.at[p],
            y * near + home,
            g,
        )

    def first_copy_same(p):
        return copy(
            packed.at[p, h],
            gathered[p].at[clus, h // near],
            first_send_same.at[p],
            first_recv.at[p],
            y * near + home,
            h,
        )

    def first_start(p):
        @pl.when(same)
        def _():
            pltpu.make_async_copy(
                packed.at[p, h], gathered[p].at[clus, h // near], first_recv.at[p]
            ).start()

        @pl.when(jnp.logical_not(same))
        def _():
            first_copy_same(p).start()

        def step(r, carry):
            first_copy(p, r).start()
            return carry

        lax.fori_loop(1, heads, step, 0)

    def q_start():
        pltpu.make_async_copy(packed_q.at[h], queries.at[h], q_recv).start()

        def step(r, carry):
            g = (h + r) % heads
            copy(packed_q.at[g], queries.at[h], q_send, q_recv, clus, g).start()
            return carry

        lax.fori_loop(1, heads, step, 0)

    def ring_cuts(p, way, step):
        if step == far:
            return (way,)
        if p == PHASES - 1 and step > 1:
            return (way, 1 - way)
        return (None,)

    def ring_ref(p, way, distance, cut):
        slot = (y + ring - distance) % ring if way == 0 else (y + distance) % ring
        if cut is None:
            return gathered[p].at[pl.ds(slot * near, near)]
        return gathered[p].at[pl.ds(slot * near + cut * (near // 2), near // 2)]

    def ring_copy(p, way, step, cut):
        ref = ring_ref(p, way, step - 1, cut)
        return copy(
            ref,
            ref,
            ring_send.at[p, way, step - 1, cut or 0],
            ring_recv.at[p, way, step - 1, cut or 0],
            above if way == 0 else below,
            h,
        )

    def ring_wait(p, way, step, cut):
        arrived(ring_ref(p, way, step, cut), ring_recv.at[p, way, step - 1, cut or 0])

    def own_copy(p, r):
        to = y * near + (u + r) % near
        return copy(
            gathered[p].at[to],
            selected[p].at[pl.ds(u * sources * tiles, tiles)],
            own_send.at[p, r - 1],
            own_recv.at[p, r - 1],
            to,
            h,
        )

    def partner_copy(p, r):
        return copy(
            staged.at[p, r - 1],
            selected[p].at[pl.ds((u * sources + 1) * tiles, (sources - 1) * tiles)],
            partner_send.at[p, r - 1],
            partner_recv.at[p, r - 1],
            y * near + (u + r) % near,
            h,
        )

    def enter(p):
        arrived(gathered[p].at[pl.ds(y * near, near)], first_recv.at[p])
        for way in range(2):
            ring_copy(p, way, 1, None).start()
        for r in range(1, near):
            own_copy(p, r).start()

    def forward(p, step, turn=None):
        for way in range(2):
            came = ring_cuts(p, way, step - 1)
            for i, cut in enumerate(ring_cuts(p, way, step)):
                if turn is None or turn == i:
                    if len(came) > 1:
                        ring_wait(p, way, step - 1, cut)
                    elif i == 0:
                        ring_wait(p, way, step - 1, None)
                    ring_copy(p, way, step, cut).start()

    def leave(p):
        for way in range(2):
            for cut in ring_cuts(p, way, far - 1)[1:]:
                ring_wait(p, way, far - 1, cut)
            ring_wait(p, way, far, way)
        for r in range(1, near):
            to = y * near + (u + r) % near
            for j in range(sources - 1):
                staged[p, r - 1, j * tiles : (j + 1) * tiles] = gathered[p][match_ref[j, to]]
            partner_copy(p, r).start()
        selected[p][pl.ds(u * sources * tiles, tiles)] = gathered[p][clus]
        for j in range(sources - 1):
            selected[p][pl.ds((u * sources + 1 + j) * tiles, tiles)] = gathered[p][
                match_ref[j, clus]
            ]

    def settle(p):
        for r in range(1, near):
            from_u = (u + near - r) % near
            arrived(
                selected[p].at[pl.ds(from_u * sources * tiles, tiles)], own_recv.at[p, r - 1]
            )
            arrived(
                selected[p].at[pl.ds((from_u * sources + 1) * tiles, (sources - 1) * tiles)],
                partner_recv.at[p, r - 1],
            )

    block_bits, near_bits = (count.bit_length() - 1 for count in (blocks, near))

    def note_blocks(b, carry):
        for n in range(chosen):
            block = pattern_ref[n, 0, b]
            source = block >> block_bits
            pair = (block & (blocks - 1)) >> 1
            tile = ((pair & (near - 1)) * sources + source) * tiles + (pair >> near_bits)
            tile_ref[b * chosen + n] = tile
            half_ref[b * chosen + n] = block & 1
        return carry

    def find(b, n):
        return tile_ref[b * chosen + n], half_ref[b * chosen + n]

    def masked(part, tile, mask):
        block = part[tile].reshape(ROWS // 16, 16, LANES)
        return (block * mask[None]).reshape(ROWS, LANES)

    def key_rows(b):
        rows = []
        for part in range(2):
            for n in range(chosen):
                tile, half = find(b, n)
                mask = masks[half]
                rows += [masked(selected[2 * i + part], tile, mask) for i in range(2)]
        return jnp.concatenate(rows, axis=0)

    def value_rows(b, side, parts):
        rows = []
        for part in parts:
            for n in range(chosen):
                tile, half = find(b, n)
                for i in range(2):
                    mask = masks[2 + 2 * half + i]
                    rows.append(masked(selected[PARTS + 2 * side + part], tile, mask))
        return jnp.concatenate(rows, axis=0)

    exponent_scale = 1.0 / (math.sqrt(HEAD_DIM) * math.log(2.0))

    def weigh(b, query, slot):
        keys = key_rows(b)
        scores[slot] = lax.dot_general(
            query, keys, (((1,), (1,)), ((), ())), preferred_element_type=jnp.float32
        )
        step = 16
        for i in range(BLOCK // step):
            s = scores[slot, i * step : (i + 1) * step, :]
            top = jnp.max(s, axis=1, keepdims=True)
            power = jnp.exp2((s - top) * exponent_scale)
            total = jnp.sum(power, axis=1, keepdims=True)
            powers[b, i * step : (i + 1) * step, :] = (power * (1.0 / total)).astype(jnp.bfloat16)

    def weigh_pair(w, carry):
        pair = queries[w]
        low, high = pair[:, :HEAD_DIM], pair[:, HEAD_DIM:]
        weigh(2 * w, jnp.concatenate([low, low], axis=1), 0)
        weigh(2 * w + 1, jnp.concatenate([high, high], axis=1), 1)
        return carry

    done = [0]

    def weigh_some(count):
        stop = min(done[0] + count, heads)
        if stop > done[0]:
            lax.fori_loop(done[0], stop, weigh_pair, 0)
        done[0] = stop

    def product(b, side, parts):
        width = chosen * BLOCK // 2
        columns = slice(parts[0] * width, (parts[-1] + 1) * width)
        return jnp.dot(
            powers[b, :, columns],
            value_rows(b, side, parts),
            preferred_element_type=jnp.float32,
        )

    def mix_ahead(i, carry):
        found = [product(4 * i + j, SIDES - 1, (0,)) for j in range(4)]
        for j in range(4):
            ahead[4 * i + j] = found[j]
        return carry

    def mix(b, side):
        if side < SIDES - 1:
            spread = product(b, side, (0, 1))
        else:
            spread = ahead[b] + product(b, side, (1,))
        spread = spread + pltpu.roll(spread, 2 * SIDE, 1)
        return spread + pltpu.roll(spread, SIDE, 1)

    def mix_pair(w, side):
        low, high = mix(2 * w, side), mix(2 * w + 1, side)
        middle = BLOCK // 2
        group = lax.broadcasted_iota(jnp.int32, (middle, LANES), 1) // SIDE
        tile = jnp.where(
            group < 2,
            jnp.where(group == 0, low[:middle], low[middle:]),
            jnp.where(group == 2, high[:middle], high[middle:]),
        )
        return tile.astype(jnp.bfloat16)

    def mix_send(w, side):
        copy(
            mixed_out.at[side, w],
            mixed_in.at[side, h],
            mixed_send.at[side],
            mixed_recv.at[side],
            clus,
            w,
        ).start()

    def mix_two(side, i, carry):
        pairs = [(h + 2 * i + j) % heads for j in (1, 2)]
        found = [mix_pair(w, side) for w in pairs]
        for w, tile in zip(pairs, found):
            mixed_out[side, w] = tile
        for w in pairs:
            mix_send(w, side)
        return carry

    mixed = [0] * SIDES

    def mix_some(side, count):
        end = heads // 2
        stop = min(mixed[side] + count, end - 1)
        if stop > mixed[side]:
            lax.fori_loop(mixed[side], stop, functools.partial(mix_two, side), 0)
        mixed[side] = stop
        if count >= end:
            other = (h + heads - 1) % heads
            found = mix_pair(other, side), mix_pair(h, side)
            mixed_out[side, other] = found[0]
            mixed_out[side, h] = found[1]
            mix_send(other, side)
            pltpu.make_async_copy(
                mixed_out.at[side, h], mixed_in.at[side, h], mixed_recv.at[side]
            ).start()

    first_start(0)
    first_start(1)
    enter(0)
    first_start(2)
    enter(1)
    first_start(3)
    loads[1].wait()
    pack(v_ref, put_values)
    forward(0, 2)
    loads[2].wait()
    pack(q_ref, put_q)
    forward(1, 2)
    first_start(4)
    forward(0, 3)
    enter(2)
    first_start(5)
    forward(0, 4)
    forward(1, 3)
    leave(0)
    forward(2, 2)
    first_start(6)
    lax.fori_loop(0, blocks, note_blocks, 0)
    forward(1, 4)
    for p in range(3, PHASES):
        enter(p)
        if p == 3:
            first_start(7)
        if p == 4:
            q_start()
        if p == PHASES - 1:
            weigh_some(2)
        forward(p - 1, 3)
        leave(p - 2)
        if p == PHASES - 2:
            for part in range(PARTS):
                settle(part)
            arrived(queries, q_recv)
        if p >= PHASES - 2:
            weigh_some(3)
        forward(p, 2)
        if p >= PHASES - 2:
            weigh_some(3)
        forward(p - 1, 4)
        if p == PHASES - 2:
            weigh_some(2)
    last = PHASES - 1
    weigh_some(heads)
    settle(PARTS)
    settle(PARTS + 1)
    mix_some(0, 1)
    forward(last, 3, 0)
    mix_some(0, 1)
    forward(last, 3, 1)
    mix_some(0, 1)
    leave(last - 1)
    mix_some(0, 1)
    forward(last, 4)
    mix_some(0, 2)
    leave(last)
    mix_some(0, heads)
    settle(last - 1)
    lax.fori_loop(0, heads // 2, mix_ahead, 0)
    settle(last)
    mix_some(1, heads)

    for p in range(PHASES):
        arrived(packed.at[p, 0 : heads - 1], first_send.at[p])

        @pl.when(jnp.logical_not(same))
        def _():
            first_copy_same(p).wait_send()

        for step in range(1, far + 1):
            for way in range(2):
                for cut in ring_cuts(p, way, step):
                    ring_copy(p, way, step, cut).wait_send()
        for r in range(1, near):
            own_copy(p, r).wait_send()
            partner_copy(p, r).wait_send()
    arrived(packed_q.at[0 : heads - 1], q_send)
    for side in range(SIDES):
        arrived(mixed_out.at[side, 0 : heads - 1], mixed_send.at[side])
        arrived(mixed_in.at[side], mixed_recv.at[side])

    step = 16
    for group in range(4):
        lanes = slice(group * SIDE, (group + 1) * SIDE)
        for i in range(BLOCK // 2 // step):
            rows = slice(i * step, (i + 1) * step)
            pieces = [
                mixed_in[side, head, rows][:, lanes]
                for head in range(heads)
                for side in range(SIDES)
            ]
            normed = jnp.concatenate(pieces, axis=1)
            at = group * (BLOCK // 2) + i * step
            out_ref[at : at + step, :] = normed.astype(out_ref.dtype)


def local(shape, node_queries, node_keys, node_values, matchings, patterns, out_gain):
    clusters, heads = shape
    near = NEAR if clusters % (8 * NEAR) == 0 else 2
    ring = clusters // near
    blocks, chosen = patterns.shape[1:]
    tiles = heads // near
    far = ring // 2
    width = node_queries.shape[1]
    dtype = node_queries.dtype
    vmem = pl.BlockSpec(memory_space=pltpu.VMEM)
    smem = pl.BlockSpec(memory_space=pltpu.SMEM)
    dma = pltpu.SemaphoreType.DMA
    scratch = [
        pltpu.VMEM(node_queries.shape, dtype),
        pltpu.VMEM(node_queries.shape, dtype),
        pltpu.VMEM(node_queries.shape, dtype),
        pltpu.VMEM((PHASES, heads, ROWS, LANES), dtype),
        pltpu.VMEM((heads, BLOCK, LANES), dtype),
        pltpu.VMEM((PHASES, near - 1, 3 * tiles, ROWS, LANES), dtype),
        pltpu.VMEM((heads, BLOCK, LANES), dtype),
        pltpu.VMEM((blocks, BLOCK, chosen * BLOCK), dtype),
        pltpu.VMEM((2, BLOCK, chosen * BLOCK), jnp.float32),
        pltpu.VMEM((6, 16, LANES), dtype),
        pltpu.VMEM((SIDES, heads, BLOCK // SIDES, LANES), dtype),
        pltpu.VMEM((SIDES, heads, BLOCK // SIDES, LANES), dtype),
        pltpu.VMEM((blocks, BLOCK, LANES), jnp.float32),
        pltpu.SMEM((blocks * chosen,), jnp.int32),
        pltpu.SMEM((blocks * chosen,), jnp.int32),
    ]
    scratch += [pltpu.VMEM((clusters, tiles, ROWS, LANES), dtype)] * PHASES
    scratch += [pltpu.VMEM((near * 4 * tiles, ROWS, LANES), dtype)] * PHASES
    scratch += [
        dma((3,)),
        dma((PHASES,)),
        dma((PHASES,)),
        dma((PHASES,)),
        dma((PHASES, 2, far, 2)),
        dma((PHASES, 2, far, 2)),
        dma((PHASES, near - 1)),
        dma((PHASES, near - 1)),
        dma((PHASES, near - 1)),
        dma((PHASES, near - 1)),
        dma,
        dma,
        dma((SIDES,)),
        dma((SIDES,)),
    ]
    rows = pl.pallas_call(
        functools.partial(attention_kernel, (heads, ring, near, chosen, blocks)),
        out_shape=jax.ShapeDtypeStruct(node_queries.shape, dtype),
        in_specs=[smem] * 2 + [pl.BlockSpec(memory_space=pl.ANY)] * 3,
        out_specs=vmem,
        scratch_shapes=scratch,
        compiler_params=pltpu.CompilerParams(
            collective_id=0, has_side_effects=True, vmem_limit_bytes=56 * 1024 * 1024
        ),
    )(
        jnp.transpose(patterns, (2, 0, 1)),
        matchings,
        node_queries,
        node_keys,
        node_values,
    ).astype(jnp.float32)
    mean_square = jnp.mean(rows * rows, axis=-1, keepdims=True)
    return (rows * lax.rsqrt(mean_square + 1e-06) * out_gain).astype(jnp.bfloat16)


def solution(mesh):
    in_specs = (
        P(("clus", "head"), None),
        P(("clus", "head"), None),
        P(("clus", "head"), None),
        P(),
        P("clus", None, None),
        P(),
    )
    out_specs = P(("clus", "head"), None)
    return jax.shard_map(
        functools.partial(local, (mesh.shape["clus"], mesh.shape["head"])),
        mesh=mesh,
        in_specs=in_specs,
        out_specs=out_specs,
        check_vma=False,
    )
```

```python
import functools
import math

import jax
import jax.numpy as jnp
from jax import lax
from jax.experimental import pallas as pl
from jax.experimental.pallas import tpu as pltpu
from jax.sharding import PartitionSpec as P

HEAD_DIM = 64
BLOCK = 128
LANES = 128
PARTS = 4
ROWS = BLOCK // PARTS
PHASES = 2 * PARTS
SIDES = 2
SIDE = HEAD_DIM // SIDES
NEAR = 4
MESH = pl.DeviceIdType.MESH


def attention_kernel(
    dims,
    pattern_ref,
    match_ref,
    q_hbm,
    k_hbm,
    v_hbm,
    out_ref,
    q_ref,
    k_ref,
    v_ref,
    packed,
    packed_q,
    staged,
    queries,
    powers,
    scores,
    masks,
    mixed_out,
    mixed_in,
    ahead,
    tile_ref,
    half_ref,
    *rest,
):
    heads, ring, near, chosen, blocks = dims
    gathered = rest[:PHASES]
    selected = rest[PHASES : 2 * PHASES]
    (
        load,
        first_send,
        first_send_same,
        first_recv,
        ring_send,
        ring_recv,
        own_send,
        own_recv,
        partner_send,
        partner_recv,
        q_send,
        q_recv,
        mixed_send,
        mixed_recv,
    ) = rest[2 * PHASES :]
    tiles = heads // near
    sources = 4
    far = ring // 2
    clus = lax.axis_index("clus")
    h = lax.axis_index("head")
    y = clus // near
    u = clus % near
    home = h % near
    same = home == u

    def copy(src, dst, send, recv, to_clus, to_head):
        return pltpu.make_async_remote_copy(
            src_ref=src,
            dst_ref=dst,
            send_sem=send,
            recv_sem=recv,
            device_id={"clus": to_clus, "head": to_head},
            device_id_type=MESH,
        )

    def far_first(r):
        return (h + heads // 2 + (r // 2) * (2 * (r % 2) - 1)) % heads

    def arrived(ref, sem):
        pltpu.make_async_copy(ref, ref, sem).wait()

    loads = [
        pltpu.make_async_copy(src, dst, load.at[i])
        for i, (src, dst) in enumerate(((k_hbm, k_ref), (v_hbm, v_ref), (q_hbm, q_ref)))
    ]
    for one in loads:
        one.start()

    barrier = pltpu.get_barrier_semaphore()

    def greet(to_clus, to_head):
        pl.semaphore_signal(
            barrier, inc=1, device_id={"clus": to_clus, "head": to_head}, device_id_type=MESH
        )

    def greet_first(i, carry):
        to_clus = y * near + i // tiles
        to_head = u + near * (i % tiles)

        @pl.when(jnp.logical_or(to_clus != clus, to_head != h))
        def _():
            greet(to_clus, to_head)

        return carry

    def greet_head(r, carry):
        greet(clus, (h + r) % heads)
        return carry

    lax.fori_loop(0, near * tiles, greet_first, 0)
    lax.fori_loop(1, heads, greet_head, 0)
    for r in range(1, near):
        greet(y * near + (u + r) % near, h)
    above = ((y + 1) % ring) * near + u
    below = ((y + ring - 1) % ring) * near + u
    greet(above, h)
    greet(below, h)

    def pack(ref, put):
        for t in range(heads // 2):
            first = ref[0:BLOCK, t * LANES : (t + 1) * LANES]
            second = ref[BLOCK : 2 * BLOCK, t * LANES : (t + 1) * LANES]
            put(
                2 * t,
                jnp.concatenate([first[:, :HEAD_DIM], second[:, :HEAD_DIM]], axis=1),
            )
            put(
                2 * t + 1,
                jnp.concatenate([first[:, HEAD_DIM:], second[:, HEAD_DIM:]], axis=1),
            )

    def put_keys(head, tile):
        for part in range(PARTS):
            packed[part, head] = tile[part * ROWS : (part + 1) * ROWS]

    def put_values(head, tile):
        middle = BLOCK // 2
        for side in range(SIDES):
            pieces = [
                tile[rows, at + side * SIDE : at + (side + 1) * SIDE]
                for at in (0, HEAD_DIM)
                for rows in (slice(0, middle), slice(middle, BLOCK))
            ]
            wide = jnp.concatenate(pieces, axis=1)
            for part in range(2):
                packed[PARTS + 2 * side + part, head] = wide[part * ROWS : (part + 1) * ROWS]

    def put_q(head, tile):
        packed_q[head] = tile

    loads[0].wait()
    pack(k_ref, put_keys)
    lane = lax.broadcasted_iota(jnp.int32, (16, LANES), 1)
    for i in range(2):
        masks[i] = jnp.where(lane // HEAD_DIM == i, 1.0, 0.0).astype(masks.dtype)
    for i in range(4):
        masks[2 + i] = jnp.where(lane // SIDE == i, 1.0, 0.0).astype(masks.dtype)

    itself = jnp.where(same, 1, 0)
    pl.semaphore_wait(barrier, (near * tiles - itself) + (heads - 1) + (near - 1) + 2)

    def first_copy(p, r):
        g = far_first(r)
        return copy(
            packed.at[p, g],
            gathered[p].at[clus, h // near],
            first_send.at[p],
            first_recv.at[p],
            y * near + home,
            g,
        )

    def first_copy_same(p):
        return copy(
            packed.at[p, h],
            gathered[p].at[clus, h // near],
            first_send_same.at[p],
            first_recv.at[p],
            y * near + home,
            h,
        )

    def first_start(p):
        @pl.when(same)
        def _():
            pltpu.make_async_copy(
                packed.at[p, h], gathered[p].at[clus, h // near], first_recv.at[p]
            ).start()

        @pl.when(jnp.logical_not(same))
        def _():
            first_copy_same(p).start()

        def step(r, carry):
            first_copy(p, r).start()
            return carry

        lax.fori_loop(1, heads, step, 0)

    def q_start():
        pltpu.make_async_copy(packed_q.at[h], queries.at[h], q_recv).start()

        def step(r, carry):
            g = far_first(r)
            copy(packed_q.at[g], queries.at[h], q_send, q_recv, clus, g).start()
            return carry

        lax.fori_loop(1, heads, step, 0)

    def ring_cuts(p, way, step):
        if step == far:
            return (way,)
        if p == PHASES - 1 and step > 1:
            return (way, 1 - way)
        return (None,)

    def ring_ref(p, way, distance, cut):
        slot = (y + ring - distance) % ring if way == 0 else (y + distance) % ring
        if cut is None:
            return gathered[p].at[pl.ds(slot * near, near)]
        return gathered[p].at[pl.ds(slot * near + cut * (near // 2), near // 2)]

    def ring_copy(p, way, step, cut):
        ref = ring_ref(p, way, step - 1, cut)
        return copy(
            ref,
            ref,
            ring_send.at[p, way, step - 1, cut or 0],
            ring_recv.at[p, way, step - 1, cut or 0],
            above if way == 0 else below,
            h,
        )

    def ring_wait(p, way, step, cut):
        arrived(ring_ref(p, way, step, cut), ring_recv.at[p, way, step - 1, cut or 0])

    def own_copy(p, r):
        to = y * near + (u + r) % near
        return copy(
            gathered[p].at[to],
            selected[p].at[pl.ds(u * sources * tiles, tiles)],
            own_send.at[p, r - 1],
            own_recv.at[p, r - 1],
            to,
            h,
        )

    def partner_copy(p, r):
        return copy(
            staged.at[p, r - 1],
            selected[p].at[pl.ds((u * sources + 1) * tiles, (sources - 1) * tiles)],
            partner_send.at[p, r - 1],
            partner_recv.at[p, r - 1],
            y * near + (u + r) % near,
            h,
        )

    def enter(p):
        arrived(gathered[p].at[pl.ds(y * near, near)], first_recv.at[p])
        for way in range(2):
            ring_copy(p, way, 1, None).start()
        for r in range(1, near):
            own_copy(p, r).start()

    def forward(p, step, turn=None):
        for way in range(2):
            came = ring_cuts(p, way, step - 1)
            for i, cut in enumerate(ring_cuts(p, way, step)):
                if turn is None or turn == i:
                    if len(came) > 1:
                        ring_wait(p, way, step - 1, cut)
                    elif i == 0:
                        ring_wait(p, way, step - 1, None)
                    ring_copy(p, way, step, cut).start()

    def leave(p):
        for way in range(2):
            for cut in ring_cuts(p, way, far - 1)[1:]:
                ring_wait(p, way, far - 1, cut)
            ring_wait(p, way, far, way)
        for r in range(1, near):
            to = y * near + (u + r) % near
            for j in range(sources - 1):
                staged[p, r - 1, j * tiles : (j + 1) * tiles] = gathered[p][match_ref[j, to]]
            partner_copy(p, r).start()
        selected[p][pl.ds(u * sources * tiles, tiles)] = gathered[p][clus]
        for j in range(sources - 1):
            selected[p][pl.ds((u * sources + 1 + j) * tiles, tiles)] = gathered[p][
                match_ref[j, clus]
            ]

    def settle(p):
        for r in range(1, near):
            from_u = (u + near - r) % near
            arrived(
                selected[p].at[pl.ds(from_u * sources * tiles, tiles)], own_recv.at[p, r - 1]
            )
            arrived(
                selected[p].at[pl.ds((from_u * sources + 1) * tiles, (sources - 1) * tiles)],
                partner_recv.at[p, r - 1],
            )

    block_bits, near_bits = (count.bit_length() - 1 for count in (blocks, near))

    def note_blocks(b, carry):
        for n in range(chosen):
            block = pattern_ref[n, 0, b]
            source = block >> block_bits
            pair = (block & (blocks - 1)) >> 1
            tile = ((pair & (near - 1)) * sources + source) * tiles + (pair >> near_bits)
            tile_ref[b * chosen + n] = tile
            half_ref[b * chosen + n] = block & 1
        return carry

    def find(b, n):
        return tile_ref[b * chosen + n], half_ref[b * chosen + n]

    def masked(part, tile, mask):
        block = part[tile].reshape(ROWS // 16, 16, LANES)
        return (block * mask[None]).reshape(ROWS, LANES)

    def key_rows(b):
        rows = []
        for part in range(2):
            for n in range(chosen):
                tile, half = find(b, n)
                mask = masks[half]
                rows += [masked(selected[2 * i + part], tile, mask) for i in range(2)]
        return jnp.concatenate(rows, axis=0)

    def value_rows(b, side, parts):
        rows = []
        for part in parts:
            for n in range(chosen):
                tile, half = find(b, n)
                for i in range(2):
                    mask = masks[2 + 2 * half + i]
                    rows.append(masked(selected[PARTS + 2 * side + part], tile, mask))
        return jnp.concatenate(rows, axis=0)

    exponent_scale = 1.0 / (math.sqrt(HEAD_DIM) * math.log(2.0))

    def weigh(b, query, slot):
        keys = key_rows(b)
        scores[slot] = lax.dot_general(
            query, keys, (((1,), (1,)), ((), ())), preferred_element_type=jnp.float32
        )
        step = 16
        for i in range(BLOCK // step):
            s = scores[slot, i * step : (i + 1) * step, :]
            top = jnp.max(s, axis=1, keepdims=True)
            power = jnp.exp2((s - top) * exponent_scale)
            total = jnp.sum(power, axis=1, keepdims=True)
            powers[b, i * step : (i + 1) * step, :] = (power * (1.0 / total)).astype(jnp.bfloat16)

    def weigh_pair(w, carry):
        pair = queries[w]
        low, high = pair[:, :HEAD_DIM], pair[:, HEAD_DIM:]
        weigh(2 * w, jnp.concatenate([low, low], axis=1), 0)
        weigh(2 * w + 1, jnp.concatenate([high, high], axis=1), 1)
        return carry

    done = [0]

    def weigh_some(count):
        stop = min(done[0] + count, heads)
        if stop > done[0]:
            lax.fori_loop(done[0], stop, weigh_pair, 0)
        done[0] = stop

    def product(b, side, parts):
        width = chosen * BLOCK // 2
        columns = slice(parts[0] * width, (parts[-1] + 1) * width)
        return jnp.dot(
            powers[b, :, columns],
            value_rows(b, side, parts),
            preferred_element_type=jnp.float32,
        )

    def mix_ahead(i, carry):
        found = [product(4 * i + j, SIDES - 1, (0,)) for j in range(4)]
        for j in range(4):
            ahead[4 * i + j] = found[j]
        return carry

    def mix(b, side):
        if side < SIDES - 1:
            spread = product(b, side, (0, 1))
        else:
            spread = ahead[b] + product(b, side, (1,))
        spread = spread + pltpu.roll(spread, 2 * SIDE, 1)
        return spread + pltpu.roll(spread, SIDE, 1)

    def mix_pair(w, side):
        low, high = mix(2 * w, side), mix(2 * w + 1, side)
        middle = BLOCK // 2
        group = lax.broadcasted_iota(jnp.int32, (middle, LANES), 1) // SIDE
        tile = jnp.where(
            group < 2,
            jnp.where(group == 0, low[:middle], low[middle:]),
            jnp.where(group == 2, high[:middle], high[middle:]),
        )
        return tile.astype(jnp.bfloat16)

    def mix_send(w, side):
        copy(
            mixed_out.at[side, w],
            mixed_in.at[side, h],
            mixed_send.at[side],
            mixed_recv.at[side],
            clus,
            w,
        ).start()

    def mix_two(side, i, carry):
        pairs = [far_first(2 * i + j) for j in (1, 2)]
        found = [mix_pair(w, side) for w in pairs]
        for w, tile in zip(pairs, found):
            mixed_out[side, w] = tile
        for w in pairs:
            mix_send(w, side)
        return carry

    mixed = [0] * SIDES

    def mix_some(side, count):
        end = heads // 2
        stop = min(mixed[side] + count, end - 1)
        if stop > mixed[side]:
            lax.fori_loop(mixed[side], stop, functools.partial(mix_two, side), 0)
        mixed[side] = stop
        if count >= end:
            other = far_first(heads - 1)
            found = mix_pair(other, side), mix_pair(h, side)
            mixed_out[side, other] = found[0]
            mixed_out[side, h] = found[1]
            mix_send(other, side)
            pltpu.make_async_copy(
                mixed_out.at[side, h], mixed_in.at[side, h], mixed_recv.at[side]
            ).start()

    first_start(0)
    first_start(1)
    enter(0)
    first_start(2)
    enter(1)
    first_start(3)
    loads[1].wait()
    pack(v_ref, put_values)
    forward(0, 2)
    loads[2].wait()
    pack(q_ref, put_q)
    forward(1, 2)
    first_start(4)
    forward(0, 3)
    enter(2)
    first_start(5)
    forward(0, 4)
    forward(1, 3)
    leave(0)
    forward(2, 2)
    first_start(6)
    lax.fori_loop(0, blocks, note_blocks, 0)
    forward(1, 4)
    for p in range(3, PHASES):
        enter(p)
        if p == 3:
            first_start(7)
        if p == 4:
            q_start()
        if p == PHASES - 1:
            weigh_some(2)
        forward(p - 1, 3)
        leave(p - 2)
        if p == PHASES - 2:
            for part in range(PARTS):
                settle(part)
            arrived(queries, q_recv)
        if p >= PHASES - 2:
            weigh_some(3)
        forward(p, 2)
        if p >= PHASES - 2:
            weigh_some(3)
        forward(p - 1, 4)
        if p == PHASES - 2:
            weigh_some(2)
    last = PHASES - 1
    weigh_some(heads)
    settle(PARTS)
    settle(PARTS + 1)
    mix_some(0, 1)
    forward(last, 3, 0)
    mix_some(0, 1)
    forward(last, 3, 1)
    mix_some(0, 1)
    leave(last - 1)
    mix_some(0, 1)
    forward(last, 4)
    mix_some(0, 2)
    leave(last)
    mix_some(0, heads)
    settle(last - 1)
    lax.fori_loop(0, heads // 2, mix_ahead, 0)
    settle(last)
    mix_some(1, heads)

    for p in range(PHASES):
        arrived(packed.at[p, 0 : heads - 1], first_send.at[p])

        @pl.when(jnp.logical_not(same))
        def _():
            first_copy_same(p).wait_send()

        for step in range(1, far + 1):
            for way in range(2):
                for cut in ring_cuts(p, way, step):
                    ring_copy(p, way, step, cut).wait_send()
        for r in range(1, near):
            own_copy(p, r).wait_send()
            partner_copy(p, r).wait_send()
    arrived(packed_q.at[0 : heads - 1], q_send)
    for side in range(SIDES):
        arrived(mixed_out.at[side, 0 : heads - 1], mixed_send.at[side])
        arrived(mixed_in.at[side], mixed_recv.at[side])

    step = 16
    for group in range(4):
        lanes = slice(group * SIDE, (group + 1) * SIDE)
        for i in range(BLOCK // 2 // step):
            rows = slice(i * step, (i + 1) * step)
            pieces = [
                mixed_in[side, head, rows][:, lanes]
                for head in range(heads)
                for side in range(SIDES)
            ]
            normed = jnp.concatenate(pieces, axis=1)
            at = group * (BLOCK // 2) + i * step
            out_ref[at : at + step, :] = normed.astype(out_ref.dtype)


def norm_kernel(rows_ref, gain_ref, out_ref):
    step = 32
    for at in range(0, rows_ref.shape[0], step):
        rows = rows_ref[at : at + step, :].astype(jnp.float32)
        mean_square = jnp.mean(rows * rows, axis=1, keepdims=True)
        normed = rows * lax.rsqrt(mean_square + 1e-06) * gain_ref[...]
        out_ref[at : at + step, :] = normed.astype(out_ref.dtype)


def local(shape, node_queries, node_keys, node_values, matchings, patterns, out_gain):
    clusters, heads = shape
    near = NEAR if clusters % (8 * NEAR) == 0 else 2
    ring = clusters // near
    blocks, chosen = patterns.shape[1:]
    tiles = heads // near
    far = ring // 2
    width = node_queries.shape[1]
    dtype = node_queries.dtype
    vmem = pl.BlockSpec(memory_space=pltpu.VMEM)
    smem = pl.BlockSpec(memory_space=pltpu.SMEM)
    dma = pltpu.SemaphoreType.DMA
    scratch = [
        pltpu.VMEM(node_queries.shape, dtype),
        pltpu.VMEM(node_queries.shape, dtype),
        pltpu.VMEM(node_queries.shape, dtype),
        pltpu.VMEM((PHASES, heads, ROWS, LANES), dtype),
        pltpu.VMEM((heads, BLOCK, LANES), dtype),
        pltpu.VMEM((PHASES, near - 1, 3 * tiles, ROWS, LANES), dtype),
        pltpu.VMEM((heads, BLOCK, LANES), dtype),
        pltpu.VMEM((blocks, BLOCK, chosen * BLOCK), dtype),
        pltpu.VMEM((2, BLOCK, chosen * BLOCK), jnp.float32),
        pltpu.VMEM((6, 16, LANES), dtype),
        pltpu.VMEM((SIDES, heads, BLOCK // SIDES, LANES), dtype),
        pltpu.VMEM((SIDES, heads, BLOCK // SIDES, LANES), dtype),
        pltpu.VMEM((blocks, BLOCK, LANES), jnp.float32),
        pltpu.SMEM((blocks * chosen,), jnp.int32),
        pltpu.SMEM((blocks * chosen,), jnp.int32),
    ]
    scratch += [pltpu.VMEM((clusters, tiles, ROWS, LANES), dtype)] * PHASES
    scratch += [pltpu.VMEM((near * 4 * tiles, ROWS, LANES), dtype)] * PHASES
    scratch += [
        dma((3,)),
        dma((PHASES,)),
        dma((PHASES,)),
        dma((PHASES,)),
        dma((PHASES, 2, far, 2)),
        dma((PHASES, 2, far, 2)),
        dma((PHASES, near - 1)),
        dma((PHASES, near - 1)),
        dma((PHASES, near - 1)),
        dma((PHASES, near - 1)),
        dma,
        dma,
        dma((SIDES,)),
        dma((SIDES,)),
    ]
    rows = pl.pallas_call(
        functools.partial(attention_kernel, (heads, ring, near, chosen, blocks)),
        out_shape=jax.ShapeDtypeStruct(node_queries.shape, dtype),
        in_specs=[smem] * 2 + [pl.BlockSpec(memory_space=pl.ANY)] * 3,
        out_specs=vmem,
        scratch_shapes=scratch,
        compiler_params=pltpu.CompilerParams(
            collective_id=0, has_side_effects=True, vmem_limit_bytes=56 * 1024 * 1024
        ),
    )(
        jnp.transpose(patterns, (2, 0, 1)),
        matchings,
        node_queries,
        node_keys,
        node_values,
    )
    return pl.pallas_call(
        norm_kernel,
        out_shape=jax.ShapeDtypeStruct(rows.shape, dtype),
        in_specs=[vmem, vmem],
        out_specs=vmem,
    )(rows, out_gain.reshape(1, width))


def solution(mesh):
    in_specs = (
        P(("clus", "head"), None),
        P(("clus", "head"), None),
        P(("clus", "head"), None),
        P(),
        P("clus", None, None),
        P(),
    )
    out_specs = P(("clus", "head"), None)
    return jax.shard_map(
        functools.partial(local, (mesh.shape["clus"], mesh.shape["head"])),
        mesh=mesh,
        in_specs=in_specs,
        out_specs=out_specs,
        check_vma=False,
    )
```

```python
import functools
import math

import jax
import jax.numpy as jnp
from jax import lax
from jax.experimental import pallas as pl
from jax.experimental.pallas import tpu as pltpu
from jax.sharding import PartitionSpec as P

HEAD_DIM = 64
BLOCK = 128
LANES = 128
PARTS = 4
ROWS = BLOCK // PARTS
PHASES = 2 * PARTS
SIDES = 2
SIDE = HEAD_DIM // SIDES
NEAR = 4
MESH = pl.DeviceIdType.MESH


def attention_kernel(
    dims,
    pattern_ref,
    match_ref,
    q_hbm,
    k_hbm,
    v_hbm,
    out_ref,
    q_ref,
    k_ref,
    v_ref,
    packed,
    packed_q,
    staged,
    queries,
    powers,
    scores,
    masks,
    mixed_out,
    mixed_in,
    ahead,
    tile_ref,
    half_ref,
    *rest,
):
    heads, ring, near, chosen, blocks = dims
    gathered = rest[:PHASES]
    selected = rest[PHASES : 2 * PHASES]
    (
        load,
        first_send,
        first_send_same,
        first_recv,
        ring_send,
        ring_recv,
        own_send,
        own_recv,
        partner_send,
        partner_recv,
        q_send,
        q_recv,
        mixed_send,
        mixed_recv,
    ) = rest[2 * PHASES :]
    tiles = heads // near
    sources = 4
    far = ring // 2
    clus = lax.axis_index("clus")
    h = lax.axis_index("head")
    y = clus // near
    u = clus % near
    home = h % near
    same = home == u

    def copy(src, dst, send, recv, to_clus, to_head):
        return pltpu.make_async_remote_copy(
            src_ref=src,
            dst_ref=dst,
            send_sem=send,
            recv_sem=recv,
            device_id={"clus": to_clus, "head": to_head},
            device_id_type=MESH,
        )

    def far_first(r):
        return (h + heads // 2 + (r // 2) * (2 * (r % 2) - 1)) % heads

    def arrived(ref, sem):
        pltpu.make_async_copy(ref, ref, sem).wait()

    loads = [
        pltpu.make_async_copy(src, dst, load.at[i])
        for i, (src, dst) in enumerate(((k_hbm, k_ref), (v_hbm, v_ref), (q_hbm, q_ref)))
    ]
    for one in loads:
        one.start()

    barrier = pltpu.get_barrier_semaphore()

    def greet(to_clus, to_head):
        pl.semaphore_signal(
            barrier, inc=1, device_id={"clus": to_clus, "head": to_head}, device_id_type=MESH
        )

    def greet_first(i, carry):
        to_clus = y * near + i // tiles
        to_head = u + near * (i % tiles)

        @pl.when(jnp.logical_or(to_clus != clus, to_head != h))
        def _():
            greet(to_clus, to_head)

        return carry

    def greet_head(r, carry):
        greet(clus, (h + r) % heads)
        return carry

    lax.fori_loop(0, near * tiles, greet_first, 0)
    lax.fori_loop(1, heads, greet_head, 0)
    for r in range(1, near):
        greet(y * near + (u + r) % near, h)
    above = ((y + 1) % ring) * near + u
    below = ((y + ring - 1) % ring) * near + u
    greet(above, h)
    greet(below, h)

    def pack(ref, put):
        for t in range(heads // 2):
            first = ref[0:BLOCK, t * LANES : (t + 1) * LANES]
            second = ref[BLOCK : 2 * BLOCK, t * LANES : (t + 1) * LANES]
            put(
                2 * t,
                jnp.concatenate([first[:, :HEAD_DIM], second[:, :HEAD_DIM]], axis=1),
            )
            put(
                2 * t + 1,
                jnp.concatenate([first[:, HEAD_DIM:], second[:, HEAD_DIM:]], axis=1),
            )

    def put_keys(head, tile):
        for part in range(PARTS):
            packed[part, head] = tile[part * ROWS : (part + 1) * ROWS]

    def put_values(head, tile):
        middle = BLOCK // 2
        for side in range(SIDES):
            pieces = [
                tile[rows, at + side * SIDE : at + (side + 1) * SIDE]
                for at in (0, HEAD_DIM)
                for rows in (slice(0, middle), slice(middle, BLOCK))
            ]
            wide = jnp.concatenate(pieces, axis=1)
            for part in range(2):
                packed[PARTS + 2 * side + part, head] = wide[part * ROWS : (part + 1) * ROWS]

    def put_q(head, tile):
        packed_q[head] = tile

    loads[0].wait()
    pack(k_ref, put_keys)
    lane = lax.broadcasted_iota(jnp.int32, (16, LANES), 1)
    for i in range(2):
        masks[i] = jnp.where(lane // HEAD_DIM == i, 1.0, 0.0).astype(masks.dtype)
    for i in range(4):
        masks[2 + i] = jnp.where(lane // SIDE == i, 1.0, 0.0).astype(masks.dtype)

    itself = jnp.where(same, 1, 0)
    pl.semaphore_wait(barrier, (near * tiles - itself) + (heads - 1) + (near - 1) + 2)

    def first_copy(p, r):
        g = far_first(r)
        return copy(
            packed.at[p, g],
            gathered[p].at[clus, h // near],
            first_send.at[p],
            first_recv.at[p],
            y * near + home,
            g,
        )

    def first_copy_same(p):
        return copy(
            packed.at[p, h],
            gathered[p].at[clus, h // near],
            first_send_same.at[p],
            first_recv.at[p],
            y * near + home,
            h,
        )

    def first_start(p):
        @pl.when(same)
        def _():
            pltpu.make_async_copy(
                packed.at[p, h], gathered[p].at[clus, h // near], first_recv.at[p]
            ).start()

        @pl.when(jnp.logical_not(same))
        def _():
            first_copy_same(p).start()

        def step(r, carry):
            first_copy(p, r).start()
            return carry

        lax.fori_loop(1, heads, step, 0)

    def q_start():
        pltpu.make_async_copy(packed_q.at[h], queries.at[h], q_recv).start()

        def step(r, carry):
            g = far_first(r)
            copy(packed_q.at[g], queries.at[h], q_send, q_recv, clus, g).start()
            return carry

        lax.fori_loop(1, heads, step, 0)

    def ring_cuts(p, way, step):
        if step == far:
            return (way,)
        if p == PHASES - 1 and step > 1:
            return (way, 1 - way)
        return (None,)

    def ring_ref(p, way, distance, cut):
        slot = (y + ring - distance) % ring if way == 0 else (y + distance) % ring
        if cut is None:
            return gathered[p].at[pl.ds(slot * near, near)]
        return gathered[p].at[pl.ds(slot * near + cut * (near // 2), near // 2)]

    def ring_copy(p, way, step, cut):
        ref = ring_ref(p, way, step - 1, cut)
        return copy(
            ref,
            ref,
            ring_send.at[p, way, step - 1, cut or 0],
            ring_recv.at[p, way, step - 1, cut or 0],
            above if way == 0 else below,
            h,
        )

    def ring_wait(p, way, step, cut):
        arrived(ring_ref(p, way, step, cut), ring_recv.at[p, way, step - 1, cut or 0])

    def own_copy(p, r):
        to = y * near + (u + r) % near
        return copy(
            gathered[p].at[to],
            selected[p].at[pl.ds(u * sources * tiles, tiles)],
            own_send.at[p, r - 1],
            own_recv.at[p, r - 1],
            to,
            h,
        )

    def partner_copy(p, r):
        return copy(
            staged.at[p, r - 1],
            selected[p].at[pl.ds((u * sources + 1) * tiles, (sources - 1) * tiles)],
            partner_send.at[p, r - 1],
            partner_recv.at[p, r - 1],
            y * near + (u + r) % near,
            h,
        )

    def enter(p):
        arrived(gathered[p].at[pl.ds(y * near, near)], first_recv.at[p])
        for way in range(2):
            ring_copy(p, way, 1, None).start()
        for r in range(1, near):
            own_copy(p, r).start()

    def forward(p, step, turn=None):
        for way in range(2):
            came = ring_cuts(p, way, step - 1)
            for i, cut in enumerate(ring_cuts(p, way, step)):
                if turn is None or turn == i:
                    if len(came) > 1:
                        ring_wait(p, way, step - 1, cut)
                    elif i == 0:
                        ring_wait(p, way, step - 1, None)
                    ring_copy(p, way, step, cut).start()

    def leave(p):
        for way in range(2):
            for cut in ring_cuts(p, way, far - 1)[1:]:
                ring_wait(p, way, far - 1, cut)
            ring_wait(p, way, far, way)
        for r in range(1, near):
            to = y * near + (u + r) % near
            for j in range(sources - 1):
                staged[p, r - 1, j * tiles : (j + 1) * tiles] = gathered[p][match_ref[j, to]]
            partner_copy(p, r).start()
        selected[p][pl.ds(u * sources * tiles, tiles)] = gathered[p][clus]
        for j in range(sources - 1):
            selected[p][pl.ds((u * sources + 1 + j) * tiles, tiles)] = gathered[p][
                match_ref[j, clus]
            ]

    def settle(p):
        for r in range(1, near):
            from_u = (u + near - r) % near
            arrived(
                selected[p].at[pl.ds(from_u * sources * tiles, tiles)], own_recv.at[p, r - 1]
            )
            arrived(
                selected[p].at[pl.ds((from_u * sources + 1) * tiles, (sources - 1) * tiles)],
                partner_recv.at[p, r - 1],
            )

    block_bits, near_bits = (count.bit_length() - 1 for count in (blocks, near))

    def note_blocks(b, carry):
        for n in range(chosen):
            block = pattern_ref[n, 0, b]
            source = block >> block_bits
            pair = (block & (blocks - 1)) >> 1
            tile = ((pair & (near - 1)) * sources + source) * tiles + (pair >> near_bits)
            tile_ref[b * chosen + n] = tile
            half_ref[b * chosen + n] = block & 1
        return carry

    def find(b, n):
        return tile_ref[b * chosen + n], half_ref[b * chosen + n]

    def masked(part, tile, mask):
        block = part[tile].reshape(ROWS // 16, 16, LANES)
        return (block * mask[None]).reshape(ROWS, LANES)

    def key_rows(b):
        rows = []
        for part in range(2):
            for n in range(chosen):
                tile, half = find(b, n)
                mask = masks[half]
                rows += [masked(selected[2 * i + part], tile, mask) for i in range(2)]
        return jnp.concatenate(rows, axis=0)

    def value_rows(b, side, parts):
        rows = []
        for part in parts:
            for n in range(chosen):
                tile, half = find(b, n)
                for i in range(2):
                    mask = masks[2 + 2 * half + i]
                    rows.append(masked(selected[PARTS + 2 * side + part], tile, mask))
        return jnp.concatenate(rows, axis=0)

    exponent_scale = 1.0 / (math.sqrt(HEAD_DIM) * math.log(2.0))

    def weigh(b, query, slot):
        keys = key_rows(b)
        scores[slot] = lax.dot_general(
            query, keys, (((1,), (1,)), ((), ())), preferred_element_type=jnp.float32
        )
        step = 16
        for i in range(BLOCK // step):
            s = scores[slot, i * step : (i + 1) * step, :]
            top = jnp.max(s, axis=1, keepdims=True)
            power = jnp.exp2((s - top) * exponent_scale)
            total = jnp.sum(power, axis=1, keepdims=True)
            powers[b, i * step : (i + 1) * step, :] = (power * (1.0 / total)).astype(jnp.bfloat16)

    def weigh_pair(w, carry):
        pair = queries[w]
        low, high = pair[:, :HEAD_DIM], pair[:, HEAD_DIM:]
        weigh(2 * w, jnp.concatenate([low, low], axis=1), 0)
        weigh(2 * w + 1, jnp.concatenate([high, high], axis=1), 1)
        return carry

    done = [0]

    def weigh_some(count):
        stop = min(done[0] + count, heads)
        if stop > done[0]:
            lax.fori_loop(done[0], stop, weigh_pair, 0)
        done[0] = stop

    def product(b, side, parts):
        width = chosen * BLOCK // 2
        columns = slice(parts[0] * width, (parts[-1] + 1) * width)
        return jnp.dot(
            powers[b, :, columns],
            value_rows(b, side, parts),
            preferred_element_type=jnp.float32,
        )

    def mix_ahead(i, carry):
        found = [product(4 * i + j, SIDES - 1, (0,)) for j in range(4)]
        for j in range(4):
            ahead[4 * i + j] = found[j]
        return carry

    def mix(b, side):
        if side < SIDES - 1:
            spread = product(b, side, (0, 1))
        else:
            spread = ahead[b] + product(b, side, (1,))
        spread = spread + pltpu.roll(spread, 2 * SIDE, 1)
        return spread + pltpu.roll(spread, SIDE, 1)

    def mix_pair(w, side):
        low, high = mix(2 * w, side), mix(2 * w + 1, side)
        middle = BLOCK // 2
        group = lax.broadcasted_iota(jnp.int32, (middle, LANES), 1) // SIDE
        tile = jnp.where(
            group < 2,
            jnp.where(group == 0, low[:middle], low[middle:]),
            jnp.where(group == 2, high[:middle], high[middle:]),
        )
        return tile.astype(jnp.bfloat16)

    def mix_send(w, side):
        copy(
            mixed_out.at[side, w],
            mixed_in.at[side, h],
            mixed_send.at[side],
            mixed_recv.at[side],
            clus,
            w,
        ).start()

    def mix_two(side, i, carry):
        pairs = [far_first(2 * i + j) for j in (2, 3)]
        found = [mix_pair(w, side) for w in pairs]
        for w, tile in zip(pairs, found):
            mixed_out[side, w] = tile
        for w in pairs:
            mix_send(w, side)
        return carry

    mixed = [0] * SIDES

    def mix_some(side, count):
        end = heads // 2
        if mixed[side] == 0:
            first = far_first(1)
            mixed_out[side, first] = mix_pair(first, side)
            mix_send(first, side)
        stop = min(mixed[side] + count, end - 1)
        if stop > mixed[side]:
            lax.fori_loop(mixed[side], stop, functools.partial(mix_two, side), 0)
        mixed[side] = stop
        if count >= end:
            mixed_out[side, h] = mix_pair(h, side)
            pltpu.make_async_copy(
                mixed_out.at[side, h], mixed_in.at[side, h], mixed_recv.at[side]
            ).start()

    first_start(0)
    first_start(1)
    enter(0)
    first_start(2)
    enter(1)
    first_start(3)
    loads[1].wait()
    pack(v_ref, put_values)
    forward(0, 2)
    loads[2].wait()
    pack(q_ref, put_q)
    forward(1, 2)
    first_start(4)
    forward(0, 3)
    enter(2)
    first_start(5)
    forward(0, 4)
    forward(1, 3)
    leave(0)
    forward(2, 2)
    first_start(6)
    lax.fori_loop(0, blocks, note_blocks, 0)
    forward(1, 4)
    for p in range(3, PHASES):
        enter(p)
        if p == 3:
            first_start(7)
        if p == 4:
            q_start()
        if p == PHASES - 1:
            weigh_some(2)
        forward(p - 1, 3)
        leave(p - 2)
        if p == PHASES - 2:
            for part in range(PARTS):
                settle(part)
            arrived(queries, q_recv)
        if p >= PHASES - 2:
            weigh_some(3)
        forward(p, 2)
        if p >= PHASES - 2:
            weigh_some(3)
        forward(p - 1, 4)
        if p == PHASES - 2:
            weigh_some(2)
    last = PHASES - 1
    weigh_some(heads)
    settle(PARTS)
    settle(PARTS + 1)
    mix_some(0, 1)
    forward(last, 3, 0)
    mix_some(0, 1)
    forward(last, 3, 1)
    mix_some(0, 1)
    leave(last - 1)
    mix_some(0, 1)
    forward(last, 4)
    mix_some(0, 2)
    leave(last)
    mix_some(0, heads)
    settle(last - 1)
    lax.fori_loop(0, heads // 2, mix_ahead, 0)
    settle(last)
    mix_some(1, heads)

    for p in range(PHASES):
        arrived(packed.at[p, 0 : heads - 1], first_send.at[p])

        @pl.when(jnp.logical_not(same))
        def _():
            first_copy_same(p).wait_send()

        for step in range(1, far + 1):
            for way in range(2):
                for cut in ring_cuts(p, way, step):
                    ring_copy(p, way, step, cut).wait_send()
        for r in range(1, near):
            own_copy(p, r).wait_send()
            partner_copy(p, r).wait_send()
    arrived(packed_q.at[0 : heads - 1], q_send)
    for side in range(SIDES):
        arrived(mixed_out.at[side, 0 : heads - 1], mixed_send.at[side])
        arrived(mixed_in.at[side], mixed_recv.at[side])

    step = 16
    for group in range(4):
        lanes = slice(group * SIDE, (group + 1) * SIDE)
        for i in range(BLOCK // 2 // step):
            rows = slice(i * step, (i + 1) * step)
            pieces = [
                mixed_in[side, head, rows][:, lanes]
                for head in range(heads)
                for side in range(SIDES)
            ]
            normed = jnp.concatenate(pieces, axis=1)
            at = group * (BLOCK // 2) + i * step
            out_ref[at : at + step, :] = normed.astype(out_ref.dtype)


def norm_kernel(rows_ref, gain_ref, out_ref):
    step = 32
    for at in range(0, rows_ref.shape[0], step):
        rows = rows_ref[at : at + step, :].astype(jnp.float32)
        mean_square = jnp.mean(rows * rows, axis=1, keepdims=True)
        normed = rows * lax.rsqrt(mean_square + 1e-06) * gain_ref[...]
        out_ref[at : at + step, :] = normed.astype(out_ref.dtype)


def local(shape, node_queries, node_keys, node_values, matchings, patterns, out_gain):
    clusters, heads = shape
    near = NEAR if clusters % (8 * NEAR) == 0 else 2
    ring = clusters // near
    blocks, chosen = patterns.shape[1:]
    tiles = heads // near
    far = ring // 2
    width = node_queries.shape[1]
    dtype = node_queries.dtype
    vmem = pl.BlockSpec(memory_space=pltpu.VMEM)
    smem = pl.BlockSpec(memory_space=pltpu.SMEM)
    dma = pltpu.SemaphoreType.DMA
    scratch = [
        pltpu.VMEM(node_queries.shape, dtype),
        pltpu.VMEM(node_queries.shape, dtype),
        pltpu.VMEM(node_queries.shape, dtype),
        pltpu.VMEM((PHASES, heads, ROWS, LANES), dtype),
        pltpu.VMEM((heads, BLOCK, LANES), dtype),
        pltpu.VMEM((PHASES, near - 1, 3 * tiles, ROWS, LANES), dtype),
        pltpu.VMEM((heads, BLOCK, LANES), dtype),
        pltpu.VMEM((blocks, BLOCK, chosen * BLOCK), dtype),
        pltpu.VMEM((2, BLOCK, chosen * BLOCK), jnp.float32),
        pltpu.VMEM((6, 16, LANES), dtype),
        pltpu.VMEM((SIDES, heads, BLOCK // SIDES, LANES), dtype),
        pltpu.VMEM((SIDES, heads, BLOCK // SIDES, LANES), dtype),
        pltpu.VMEM((blocks, BLOCK, LANES), jnp.float32),
        pltpu.SMEM((blocks * chosen,), jnp.int32),
        pltpu.SMEM((blocks * chosen,), jnp.int32),
    ]
    scratch += [pltpu.VMEM((clusters, tiles, ROWS, LANES), dtype)] * PHASES
    scratch += [pltpu.VMEM((near * 4 * tiles, ROWS, LANES), dtype)] * PHASES
    scratch += [
        dma((3,)),
        dma((PHASES,)),
        dma((PHASES,)),
        dma((PHASES,)),
        dma((PHASES, 2, far, 2)),
        dma((PHASES, 2, far, 2)),
        dma((PHASES, near - 1)),
        dma((PHASES, near - 1)),
        dma((PHASES, near - 1)),
        dma((PHASES, near - 1)),
        dma,
        dma,
        dma((SIDES,)),
        dma((SIDES,)),
    ]
    rows = pl.pallas_call(
        functools.partial(attention_kernel, (heads, ring, near, chosen, blocks)),
        out_shape=jax.ShapeDtypeStruct(node_queries.shape, dtype),
        in_specs=[smem] * 2 + [pl.BlockSpec(memory_space=pl.ANY)] * 3,
        out_specs=vmem,
        scratch_shapes=scratch,
        compiler_params=pltpu.CompilerParams(
            collective_id=0, has_side_effects=True, vmem_limit_bytes=56 * 1024 * 1024
        ),
    )(
        jnp.transpose(patterns, (2, 0, 1)),
        matchings,
        node_queries,
        node_keys,
        node_values,
    )
    return pl.pallas_call(
        norm_kernel,
        out_shape=jax.ShapeDtypeStruct(rows.shape, dtype),
        in_specs=[vmem, vmem],
        out_specs=vmem,
    )(rows, out_gain.reshape(1, width))


def solution(mesh):
    in_specs = (
        P(("clus", "head"), None),
        P(("clus", "head"), None),
        P(("clus", "head"), None),
        P(),
        P("clus", None, None),
        P(),
    )
    out_specs = P(("clus", "head"), None)
    return jax.shard_map(
        functools.partial(local, (mesh.shape["clus"], mesh.shape["head"])),
        mesh=mesh,
        in_specs=in_specs,
        out_specs=out_specs,
        check_vma=False,
    )
```
